32 devices in a mesh: grp: 2 (over x), lon: 8 (over z, y), lat: 2 (over core).
Axes of the slice: x: 2, y: 2, z: 4, core: 2. Of those that a mesh axis runs over, the one named last changes fastest.
Arguments:
- cloud_state: float32 [4, 256, 128, 1024], P('grp', 'lon', 'lat'), parts along dimension 0, may hold values from -6 to 6
- counts: int32 [512, 128], P(('grp', 'lon'), 'lat'), parts along dimension 0, may hold values from 1 to 8, as said below
- courant: float32 [32], replicated, may hold values from 0.2 to 0.9
- truncation: int32 [96], replicated, may hold values from 0 to 94, as said below
Outputs:
- cloud_next: float32 [4, 256, 128, 1024], P('grp', 'lon', 'lat'), parts along dimension 0
The draws below stay inside these ranges and needn't reach their ends.
There are 2 independent parts, one for each index of `grp`. The reference program is written for one: setup_inputs(seed, part) draws one part's arguments, and reference() takes and returns one part's arrays. A program takes and returns all parts, laid end to end along the dimension named above; an argument that names none is the same for every part. Nothing has to cross between parts.
Inputs may be any that keep to these rules, and one draw needn't show every extreme that they name: `counts`: columns come in busy regions of 4 to 8 substeps and calm ones of 1 or 2; column 0, 0 has 8. truncation[m] lies in m .. 85 for m <= 85, truncation[0] = 85, and truncation[m] = m - 1 (nothing kept) for m > 85.
All inputs are finite; a program needn't handle non-finite values.
Results may differ from the reference program's by a relative error of at most 0.0003.
Values sent between devices are 32-bit elements; how exact they have to be, the bound alone decides.
A program may use at most 64 MiB of HBM per device.

```python
import jax
import jax.numpy as jnp
from jax import lax

NLON = 256
NLAT = 128
NCX = 32
NLEV = 32
MW = 96
NN = 96
NT = 85
SMAX = 8


def draw_counts(key, part):
    keys = jax.random.split(key, 4)
    lon_rows = jnp.arange(NLON)[:, None]
    lat_rows = jnp.arange(NLAT)[None, :]
    region = lon_rows // (NLON // 16) * 2 + lat_rows // (NLAT // 2)
    intensity = jax.random.randint(keys[0], (32,), 0, 5)
    group = lon_rows // max(NLON // 128, 1) * 2 + lat_rows // (NLAT // 2)
    chance = jax.random.randint(keys[1], (256,), 0, 4)
    stormy = chance[group] < intensity[region]
    busy = jax.random.randint(keys[2], (NLON, NLAT), 4, SMAX + 1)
    entries = jax.random.randint(keys[3], (NLON, NLAT), 1, 3)
    values = jnp.where(stormy, busy, entries)
    return values.at[0, 0].set(SMAX).astype(jnp.int32)


def draw_truncation(key, part):
    modes = jnp.arange(MW)
    lowest = jnp.minimum(modes, NT)
    drawn = jax.random.randint(key, (MW,), lowest, NT + 1)
    values = jnp.where(modes <= NT, drawn, modes - 1)
    return values.at[0].set(NT).astype(jnp.int32)


def block_scale(own_key, extent, pieces, low, high):
    gain, own = 1.0, jax.random.fold_in(own_key, 6)
    for axis_at, shards_of in pieces:
        heights = jnp.exp(jax.random.uniform(jax.random.fold_in(own, axis_at), (shards_of,), jnp.float32, low / len(pieces), high / len(pieces)))
        gain = gain * jnp.repeat(heights, extent[axis_at] // shards_of).reshape([-1 if axis == axis_at else 1 for axis in range(len(extent))])
    return gain


def gaussian(own_key, dims, deviation, most, shards=(), held_as=jnp.bfloat16):
    loudness = block_scale(own_key, dims, shards, -0.22, 0.18) if shards else 1.0
    entries = jax.random.normal(own_key, dims, jnp.float32) * deviation * loudness
    return jnp.minimum(jnp.maximum(entries, -most), most).astype(held_as)


def setup_inputs(seed: int = 0, part: int = 0) -> dict:
    seeds = jax.random.split(jax.random.key(seed), 5)
    part_splits = jax.random.split(jax.random.fold_in(seeds[4], part), 5)
    cloud_state = gaussian(part_splits[0], (2, NLON, NLAT, NCX * NLEV), 1.0, 6.0, ((1, 8), (2, 2)), jnp.float32)
    counts = draw_counts(jax.random.fold_in(jax.random.fold_in(seeds[4], part), 71), part)
    courant = jnp.clip(jax.random.uniform(seeds[2], (NLEV,), jnp.float32, 0.2, 0.9), 0.2, 0.9)
    truncation = draw_truncation(jax.random.fold_in(seeds[4], 71), part)
    return dict(cloud_state=cloud_state, counts=counts, courant=courant, truncation=truncation)


couple_gain = 8.0

def legendre(orders, lat_rows, lat_total, degrees):
    latitude = -0.5 * jnp.pi + jnp.pi * (lat_rows.astype(jnp.float32) + 0.5) / lat_total
    sin_lat = jnp.sin(latitude)
    cos_lat = jnp.cos(latitude)
    order_f = orders.astype(jnp.float32)
    ladder = jnp.arange(1, degrees + 1).astype(jnp.float32)
    log_gains = 0.5 * jnp.log((2.0 * ladder + 1.0) / (2.0 * ladder))
    included = (ladder[None, :] <= order_f[:, None]).astype(jnp.float32)
    log_start = 0.5 * jnp.log(jnp.float32(0.5)) + lax.optimization_barrier(jnp.sum(included * log_gains[None, :], axis=1))
    diagonal = jnp.exp(log_start[:, None] + order_f[:, None] * jnp.log(cos_lat)[None, :])

    def advance(carry, degree):
        previous, earlier, inverse = carry
        degree_f = degree.astype(jnp.float32)
        higher = degree_f > order_f
        numerator = jnp.maximum(4.0 * degree_f * degree_f - 1.0, 1.0)
        denominator = jnp.where(higher, degree_f * degree_f - order_f * order_f, 1.0)
        factor = jnp.sqrt(numerator / denominator)
        raised = factor[:, None] * (sin_lat[None, :] * previous - inverse[:, None] * earlier)
        current = jnp.where((degree_f == order_f)[:, None], diagonal, jnp.where(higher[:, None], raised, 0.0))
        return ((current, previous, jnp.where(higher, 1.0 / factor, 0.0)), current)
    initial = (jnp.zeros_like(diagonal), jnp.zeros_like(diagonal), jnp.zeros_like(order_f))
    _, stacked = lax.scan(advance, initial, jnp.arange(degrees, dtype=jnp.int32), unroll=8)
    return jnp.transpose(stacked, (1, 0, 2))

def latitude_weights(lat_rows, lat_total):
    latitude = -0.5 * jnp.pi + jnp.pi * (lat_rows.astype(jnp.float32) + 0.5) / lat_total
    return jnp.pi * jnp.cos(latitude) / lat_total

def wave_table(lon_rows, modes, lon_total):
    phase = lon_rows[:, None] * modes[None, :] % lon_total
    angle = phase.astype(jnp.float32) * (2.0 * jnp.pi / lon_total)
    return (jnp.cos(angle), jnp.sin(angle))

def substep(theta, moist, force, count, index, rate, profile, levels):
    heated = theta + couple_gain * profile[None, None, :] * force[:, :, None]
    moved_theta = heated - rate * (heated - jnp.roll(heated, levels, axis=2))
    moved_moist = moist - rate * (moist - jnp.roll(moist, levels, axis=2))
    excess = moved_moist - (1.0 + 0.2 * moved_theta)
    condensed = 0.25 * (excess + jnp.sqrt(excess * excess + 0.01))
    active = (index < count)[:, :, None]
    return (jnp.where(active, moved_theta + 0.5 * condensed, theta), jnp.where(active, moved_moist - condensed, moist))

def reference(cloud_state, counts, courant, truncation):
    highest = lax.Precision.HIGHEST
    heating = lax.optimization_barrier(jnp.mean(cloud_state[0], axis=2))
    lon_rows = jnp.arange(NLON, dtype=jnp.int32)
    modes = jnp.arange(MW, dtype=jnp.int32)
    cosine_table, sine_table = wave_table(lon_rows, modes, NLON)
    coefs = jnp.stack([jnp.dot(cosine_table.T, heating, precision=highest), jnp.dot(sine_table.T, heating, precision=highest)], 1) / NLON
    lat_rows = jnp.arange(NLAT, dtype=jnp.int32)
    table = legendre(modes, lat_rows, NLAT, NN)
    weights = latitude_weights(lat_rows, NLAT)
    spectrum = jnp.einsum('mnj,mcj->mcn', table, coefs * weights[None, None, :], precision=highest)
    degrees = jnp.arange(NN, dtype=jnp.int32)
    keep_mask = ((degrees[None, :] >= modes[:, None]) & (degrees[None, :] <= truncation[:, None])).astype(jnp.float32)
    filtered = jnp.einsum('mnj,mcn->mcj', table, spectrum * keep_mask[:, None, :], precision=highest)
    factor = jnp.where(modes == 0, 1.0, 2.0).astype(jnp.float32)[:, None]
    forcing = jnp.dot(cosine_table, factor * filtered[:, 0], precision=highest) + jnp.dot(sine_table, factor * filtered[:, 1], precision=highest)
    level_profile = jnp.sin(jnp.pi * (jnp.arange(NLEV).astype(jnp.float32) + 0.5) / NLEV)
    profile = jnp.tile(level_profile, NCX)
    rate = jnp.tile(courant, NCX)[None, None, :]
    theta = cloud_state[0]
    moist = cloud_state[1]
    for substep_index in range(SMAX):
        theta, moist = substep(theta, moist, forcing, counts, substep_index, rate, profile, NLEV)
    return jnp.stack([theta, moist])
```

```python
import functools

import jax
import jax.numpy as jnp
import numpy as np
from jax import lax
from jax.experimental import pallas as pl
from jax.experimental.pallas import tpu as pltpu
from jax.sharding import PartitionSpec as P

NN = 96
COUPLE = 8.0
HIGHEST = lax.Precision.HIGHEST
MESH = pl.DeviceIdType.MESH


def wave_tables(total_lon, lon_devices, modes, peers, scale):
    per_peer = modes // peers
    lon_local = total_lon // lon_devices
    rows = np.zeros((peers, 2, 8, total_lon))
    back = np.zeros((peers, 2, 8, total_lon))
    lons = np.arange(total_lon)
    for peer in range(peers):
        for at in range(per_peer):
            mode = peer * per_peer + at
            angle = 2.0 * np.pi * ((lons * mode) % total_lon) / total_lon
            rows[peer, 0, at], rows[peer, 1, at] = np.cos(angle), np.sin(angle)
            back[peer, :, at] = rows[peer, :, at] * (1.0 if mode == 0 else 2.0)
    rows = rows.reshape(peers * 16, lon_devices, lon_local).transpose(1, 0, 2) * scale
    back = back.reshape(peers * 16, lon_devices, lon_local).transpose(1, 2, 0)
    return rows.astype(np.float32), back.astype(np.float32)


def latitude_rows(total_lat):
    latitude = -0.5 * np.pi + np.pi * (np.arange(total_lat) + 0.5) / total_lat
    cosine = np.cos(latitude)
    rows = np.stack([np.sin(latitude), np.pi * cosine / total_lat, np.log(cosine)])
    return np.repeat(rows[:, None, :], 8, axis=1).astype(np.float32)


def order_starts(modes, total_lat):
    ladder = np.arange(1, modes + 8)
    gains = np.concatenate([[0.0], np.cumsum(0.5 * np.log((2.0 * ladder + 1.0) / (2.0 * ladder)))])
    return np.repeat((0.5 * np.log(0.5) + gains)[:, None], total_lat, axis=1).astype(np.float32)


def spectral_kernel(
    lon_devices, lat_devices, modes, chunks,
    trunc_ref, state_ref, forward_ref, back_ref, lat_ref, start_ref, out_ref,
    theta, table, heat, forward, back, send1, recv1, send2, recv2,
    load_sem, table_sem, s1_sem, r1_sem, s2_sem, r2_sem,
):
    grp = lax.axis_index("grp")
    lon = lax.axis_index("lon")
    lat = lax.axis_index("lat")
    peers = lon_devices * lat_devices
    per_peer = modes // peers
    me = lon * lat_devices + lat
    lon_local, lat_local, cells = theta.shape
    rows = lon_local // chunks

    def theta_copy(chunk):
        span = pl.ds(chunk * rows, rows)
        return pltpu.make_async_copy(state_ref.at[0, span], theta.at[span], load_sem.at[chunk])

    for chunk in range(chunks):
        theta_copy(chunk).start()
    forward_copy = pltpu.make_async_copy(forward_ref.at[lon], forward, table_sem.at[0])
    back_copy = pltpu.make_async_copy(back_ref.at[lon], back, table_sem.at[1])
    forward_copy.start()
    back_copy.start()

    barrier = pltpu.get_barrier_semaphore()

    def place(offset):
        peer = lax.rem(me + offset, peers)
        return peer, (grp, peer // lat_devices, lax.rem(peer, lat_devices))

    def greet(offset, carry):
        _, device = place(offset)
        pl.semaphore_signal(barrier, inc=1, device_id=device, device_id_type=MESH)
        return carry

    lax.fori_loop(1, peers, greet, 0)

    total_lat = table.shape[1]
    sin_lat = lat_ref[0]
    weight = lat_ref[1]
    order_f = (me * per_peer + lax.broadcasted_iota(jnp.int32, (8, total_lat), 0)).astype(jnp.float32)
    start = jnp.concatenate(
        [start_ref[pl.ds(me * per_peer + at, 1), :] for at in range(8)], axis=0
    )
    diagonal = jnp.exp(start + order_f * lat_ref[2])
    zero = jnp.zeros((8, total_lat), jnp.float32)

    def rung(degree_f, carry):
        previous, earlier, inverse = carry
        higher = degree_f > order_f
        numerator = jnp.maximum(4.0 * degree_f * degree_f - 1.0, 1.0)
        denominator = jnp.where(higher, degree_f * degree_f - order_f * order_f, 1.0)
        factor = jnp.sqrt(numerator / denominator)
        back_factor = jnp.sqrt(denominator / numerator)
        raised = factor * (sin_lat * previous - inverse * earlier)
        current = jnp.where(degree_f == order_f, diagonal, jnp.where(higher, raised, 0.0))
        return current, previous, jnp.where(higher, back_factor, 0.0)

    def ladder(block, carry):
        for at in range(8):
            degree = block * 8 + at
            carry = rung(degree.astype(jnp.float32), carry)
            table[pl.ds(pl.multiple_of(degree * 8, 8), 8), :] = carry[0]
        return carry

    lax.fori_loop(0, NN // 8, ladder, (zero, zero, zero))

    ones = jnp.ones((8, 128), jnp.float32)
    for chunk in range(chunks):
        theta_copy(chunk).wait()

        def add_row(at, carry):
            row = chunk * rows + at
            total = theta[row, :, 0:128]
            for tile in range(1, cells // 128):
                total = total + theta[row, :, tile * 128:(tile + 1) * 128]
            heat[row] = lax.dot_general(
                ones, total, (((1,), (1,)), ((), ())),
                precision=HIGHEST, preferred_element_type=jnp.float32,
            )
            return carry

        lax.fori_loop(0, rows, add_row, 0)
    forward_copy.wait()
    back_copy.wait()
    heating = heat[:, 0, :]
    coefs = jnp.dot(forward[...], heating, precision=HIGHEST, preferred_element_type=jnp.float32)
    send1[...] = coefs.reshape(peers, 16, lat_local)
    pl.semaphore_wait(barrier, peers - 1)

    def first(offset):
        peer, device = place(offset)
        return pltpu.make_async_remote_copy(
            src_ref=send1.at[peer], dst_ref=recv1.at[me],
            send_sem=s1_sem.at[peer], recv_sem=r1_sem.at[me],
            device_id=device, device_id_type=MESH,
        )

    def first_arrival(offset):
        peer, device = place(offset)
        return pltpu.make_async_remote_copy(
            src_ref=send1.at[peer], dst_ref=recv1.at[peer],
            send_sem=s1_sem.at[peer], recv_sem=r1_sem.at[peer],
            device_id=device, device_id_type=MESH,
        )

    def second(offset):
        peer, device = place(offset)
        return pltpu.make_async_remote_copy(
            src_ref=send2.at[lax.rem(peer, lat_devices)], dst_ref=recv2.at[me],
            send_sem=s2_sem.at[peer], recv_sem=r2_sem.at[me],
            device_id=device, device_id_type=MESH,
        )

    def second_arrival(offset):
        peer, device = place(offset)
        return pltpu.make_async_remote_copy(
            src_ref=send2.at[lax.rem(peer, lat_devices)], dst_ref=recv2.at[peer],
            send_sem=s2_sem.at[peer], recv_sem=r2_sem.at[peer],
            device_id=device, device_id_type=MESH,
        )

    def for_peers(act):
        def step(offset, carry):
            act(offset)
            return carry
        lax.fori_loop(1, peers, step, 0)

    for_peers(lambda offset: first(offset).start())
    recv1[me] = send1[me]
    for_peers(lambda offset: first_arrival(offset).wait_recv())
    halves = []
    for half in range(lat_devices):
        total = recv1[half]
        for at in range(1, lon_devices):
            total = total + recv1[at * lat_devices + half]
        halves.append(total)
    whole = jnp.concatenate(halves, axis=1)
    weighted = whole * jnp.concatenate([weight, weight], axis=0)

    width = table.shape[0]
    spectrum = lax.dot_general(
        weighted, table[...], (((1,), (1,)), ((), ())),
        precision=HIGHEST, preferred_element_type=jnp.float32,
    )
    lane = lax.broadcasted_iota(jnp.int32, (16, width), 1)
    own = lax.rem(lax.broadcasted_iota(jnp.int32, (16, width), 0), 8)
    kept = jnp.full((16, width), -1, jnp.int32)
    for at in range(per_peer):
        kept = jnp.where(own == at, trunc_ref[me * per_peer + at], kept)
    keep = (lane % 8 == own) & (lane // 8 <= kept)
    filtered = jnp.dot(
        jnp.where(keep, spectrum, 0.0), table[...],
        precision=HIGHEST, preferred_element_type=jnp.float32,
    )
    for half in range(lat_devices):
        send2[half] = filtered[:, half * lat_local:(half + 1) * lat_local]
    for_peers(lambda offset: second(offset).start())
    recv2[me] = send2[lat]
    for_peers(lambda offset: second_arrival(offset).wait_recv())
    gathered = recv2[...].reshape(peers * 16, lat_local)
    out_ref[...] = jnp.dot(
        back[...], gathered, precision=HIGHEST, preferred_element_type=jnp.float32
    )
    for_peers(lambda offset: first(offset).wait_send())
    for_peers(lambda offset: second(offset).wait_send())


def spectral_forcing(cloud_state, truncation):
    lon_devices = lax.axis_size("lon")
    lat_devices = lax.axis_size("lat")
    peers = lon_devices * lat_devices
    _, lon_local, lat_local, cells = cloud_state.shape
    total_lon, total_lat = lon_local * lon_devices, lat_local * lat_devices
    modes = truncation.shape[0]
    chunks = 8 if lon_local % 8 == 0 else 1
    forward, back = wave_tables(total_lon, lon_devices, modes, peers, 1.0 / (total_lon * cells))
    lat_consts = latitude_rows(total_lat)
    starts = order_starts(modes, total_lat)
    vmem = pl.BlockSpec(memory_space=pltpu.VMEM)
    hbm = pl.BlockSpec(memory_space=pl.ANY)
    return pl.pallas_call(
        functools.partial(spectral_kernel, lon_devices, lat_devices, modes, chunks),
        out_shape=jax.ShapeDtypeStruct((lon_local, lat_local), jnp.float32),
        in_specs=[pl.BlockSpec(memory_space=pltpu.SMEM), hbm, hbm, hbm, vmem, vmem],
        out_specs=vmem,
        scratch_shapes=[
            pltpu.VMEM((lon_local, lat_local, cells), jnp.float32),
            pltpu.VMEM((NN * 8, total_lat), jnp.float32),
            pltpu.VMEM((lon_local, 8, lat_local), jnp.float32),
            pltpu.VMEM(forward.shape[1:], jnp.float32),
            pltpu.VMEM(back.shape[1:], jnp.float32),
            pltpu.VMEM((peers, 16, lat_local), jnp.float32),
            pltpu.VMEM((peers, 16, lat_local), jnp.float32),
            pltpu.VMEM((lat_devices, 16, lat_local), jnp.float32),
            pltpu.VMEM((peers, 16, lat_local), jnp.float32),
            pltpu.SemaphoreType.DMA((chunks,)),
            pltpu.SemaphoreType.DMA((2,)),
            pltpu.SemaphoreType.DMA((peers,)),
            pltpu.SemaphoreType.DMA((peers,)),
            pltpu.SemaphoreType.DMA((peers,)),
            pltpu.SemaphoreType.DMA((peers,)),
        ],
        compiler_params=pltpu.CompilerParams(
            collective_id=0, has_side_effects=True, vmem_limit_bytes=24 << 20
        ),
        name="spectral",
    )(truncation, cloud_state, jnp.asarray(forward), jnp.asarray(back), jnp.asarray(lat_consts), jnp.asarray(starts))


BATCH = 16


def swap_blocks(cols, low_half, even):
    a0 = jnp.where(low_half, cols[0], pltpu.roll(cols[2], 64, 1))
    b0 = jnp.where(low_half, pltpu.roll(cols[0], 64, 1), cols[2])
    a1 = jnp.where(low_half, cols[1], pltpu.roll(cols[3], 64, 1))
    b1 = jnp.where(low_half, pltpu.roll(cols[1], 64, 1), cols[3])
    return [
        jnp.where(even, a0, pltpu.roll(a1, 32, 1)),
        jnp.where(even, pltpu.roll(a0, 96, 1), a1),
        jnp.where(even, b0, pltpu.roll(b1, 32, 1)),
        jnp.where(even, pltpu.roll(b0, 96, 1), b1),
    ]


def cloud_kernel(lat_local, counts_ref, force_ref, const_ref, x_ref, o_ref):
    chunk = pl.program_id(0)
    blocks = x_ref.shape[1]
    rows = blocks * 8 // lat_local
    lane = lax.broadcasted_iota(jnp.int32, (8, 128), 1)
    low_half = lane < 64
    even = (lane // 32) % 2 == 0
    kappa = 0.275 / 0.725

    def batch(index, carry):
        spots = []
        for at in range(BATCH):
            column = index * BATCH + at
            row, lat = column // lat_local, column % lat_local
            spots.append((column // 8, column % 8, chunk * rows + row, lat))
        counts = [counts_ref[spot[2], spot[3]] for spot in spots]
        forces = [force_ref[spot[2], spot[3]] for spot in spots]
        most = functools.reduce(jnp.maximum, counts)
        rho = const_ref[0]
        profile = const_ref[1]
        us, ws, heats, trips = [], [], [], []
        for group in range(BATCH // 4):
            u4, w4 = [], []
            for at in range(group * 4, group * 4 + 4):
                block, sub = spots[at][0], spots[at][1]
                theta = x_ref[0, block, pl.ds(sub, 8, stride=8), :]
                moist = x_ref[1, block, pl.ds(sub, 8, stride=8), :]
                u4.append((10.0 / 0.725) * moist - (2.0 / 0.725) * theta - (10.0 / 0.725))
                w4.append(theta + 0.5 * moist)
            us += swap_blocks(u4, low_half, even)
            ws += swap_blocks(w4, low_half, even)

            def spread(values):
                first = jnp.where(even, values[0], values[1])
                second = jnp.where(even, values[2], values[3])
                return jnp.where(low_half, first, second)

            heats.append(spread(forces[group * 4:group * 4 + 4]) * profile)
            trips.append(spread(counts[group * 4:group * 4 + 4]))

        def advance(step, state):
            us, ws = state
            scale = const_ref[2 + 9 + step + 1]
            floor = scale * scale
            next_us, next_ws = [], []
            for group in range(BATCH // 4):
                active = step < trips[group]
                push = 2.0 * heats[group] * scale
                u4 = us[group * 4:group * 4 + 4]
                w4 = ws[group * 4:group * 4 + 4]
                u_before = [pltpu.roll(u4[3], 1, 0)] + list(u4[:3])
                w_before = [pltpu.roll(w4[3], 1, 0)] + list(w4[:3])
                for at in range(4):
                    y = u4[at] + rho * u_before[at] - push
                    z = y * y + floor
                    root = z * lax.rsqrt(z)
                    next_us.append(jnp.where(active, y - kappa * root, u4[at]))
                    next_ws.append(jnp.where(active, w4[at] + rho * w_before[at], w4[at]))
            return tuple(next_us), tuple(next_ws)

        us, ws = lax.fori_loop(0, most, advance, (tuple(us), tuple(ws)))

        for group in range(BATCH // 4):
            def spread_rows(base):
                rows4 = [const_ref[base + counts[group * 4 + at]] for at in range(4)]
                return jnp.where(
                    low_half, jnp.where(even, rows4[0], rows4[1]), jnp.where(even, rows4[2], rows4[3])
                )

            u_scale = spread_rows(2 + 18)
            w_scale = spread_rows(2)
            shift = trips[group].astype(jnp.float32) * heats[group] * (1.0 / 1.1) - 0.5 / 1.1
            u_theta = u_scale * (0.5 / 1.1)
            thetas, moists = [], []
            for at in range(4):
                u, w = us[group * 4 + at], ws[group * 4 + at]
                theta = w_scale * w - u_theta * u + shift
                thetas.append(theta)
                moists.append(u_scale * u + (1.0 + 0.2 * theta))
            thetas = swap_blocks(thetas, low_half, even)
            moists = swap_blocks(moists, low_half, even)
            for at in range(4):
                block, sub = spots[group * 4 + at][0], spots[group * 4 + at][1]
                o_ref[0, block, pl.ds(sub, 8, stride=8), :] = thetas[at]
                o_ref[1, block, pl.ds(sub, 8, stride=8), :] = moists[at]
        return carry

    lax.fori_loop(0, blocks * 8 // BATCH, batch, 0)


def cloud_constants(courant, levels):
    rate = jnp.tile(courant, 128 // levels)
    level = jnp.tile(jnp.sin(jnp.pi * (jnp.arange(levels).astype(jnp.float32) + 0.5) / levels), 128 // levels)
    keep = 1.0 - rate
    lower = 0.725 * keep
    inverse = 1.0 / lower

    def powers(base, first):
        out = [first]
        for _ in range(8):
            out.append(out[-1] * base)
        return out

    one = jnp.ones_like(rate)
    rows = [rate / keep, COUPLE * level]
    rows += powers(keep, one / 1.1) + powers(inverse, one) + powers(lower, one * 0.0725)
    return jnp.broadcast_to(jnp.stack(rows)[:, None, :], (len(rows), 8, 128))


def shards(cloud_state, counts, courant, truncation):
    fields, lon_local, lat_local, cells = cloud_state.shape
    levels = courant.shape[0]
    forcing = spectral_forcing(cloud_state, truncation)
    consts = cloud_constants(courant, levels)
    lat_blocks, tiles = lat_local // 8, cells // 128
    view = cloud_state.reshape(fields, lon_local, lat_blocks, 8, tiles, 128)
    view = view.transpose(0, 1, 2, 4, 3, 5).reshape(fields, lon_local * lat_blocks, tiles * 8, 128)
    rows = 4 if lon_local % 4 == 0 else 1
    block = pl.BlockSpec((fields, rows * lat_blocks, tiles * 8, 128), lambda i: (0, i, 0, 0))
    smem = pl.BlockSpec(memory_space=pltpu.SMEM)
    updated = pl.pallas_call(
        functools.partial(cloud_kernel, lat_local),
        out_shape=jax.ShapeDtypeStruct(view.shape, jnp.float32),
        grid=(lon_local // rows,),
        in_specs=[smem, smem, pl.BlockSpec(memory_space=pltpu.VMEM), block],
        out_specs=block,
        compiler_params=pltpu.CompilerParams(vmem_limit_bytes=24 << 20),
        name="cloud",
    )(counts, forcing, consts, view)
    updated = updated.reshape(fields, lon_local, lat_blocks, tiles, 8, 128).transpose(0, 1, 2, 4, 3, 5)
    return updated.reshape(cloud_state.shape)


def solution(mesh):
    return jax.shard_map(
        shards,
        mesh=mesh,
        in_specs=(P("grp", "lon", "lat", None), P(("grp", "lon"), "lat"), P(), P()),
        out_specs=P("grp", "lon", "lat", None),
        check_vma=False,
    )
```

```python
import functools

import jax
import jax.numpy as jnp
import numpy as np
from jax import lax
from jax.experimental import pallas as pl
from jax.experimental.pallas import tpu as pltpu
from jax.sharding import PartitionSpec as P

NN = 96
COUPLE = 8.0
HIGHEST = lax.Precision.HIGHEST
MESH = pl.DeviceIdType.MESH


def wave_tables(total_lon, lon_devices, modes, peers, scale):
    per_peer = modes // peers
    lon_local = total_lon // lon_devices
    rows = np.zeros((peers, 2, 8, total_lon))
    back = np.zeros((peers, 2, 8, total_lon))
    lons = np.arange(total_lon)
    for peer in range(peers):
        for at in range(per_peer):
            mode = peer * per_peer + at
            angle = 2.0 * np.pi * ((lons * mode) % total_lon) / total_lon
            rows[peer, 0, at], rows[peer, 1, at] = np.cos(angle), np.sin(angle)
            back[peer, :, at] = rows[peer, :, at] * (1.0 if mode == 0 else 2.0)
    rows = rows.reshape(peers * 16, lon_devices, lon_local).transpose(1, 0, 2) * scale
    back = back.reshape(peers * 16, lon_devices, lon_local).transpose(1, 2, 0)
    return rows.astype(np.float32), back.astype(np.float32)


def latitude_rows(total_lat):
    latitude = -0.5 * np.pi + np.pi * (np.arange(total_lat) + 0.5) / total_lat
    cosine = np.cos(latitude)
    rows = np.stack([np.sin(latitude), np.pi * cosine / total_lat, np.log(cosine)])
    return np.repeat(rows[:, None, :], 8, axis=1).astype(np.float32)


def order_starts(modes, total_lat):
    ladder = np.arange(1, modes + 8)
    gains = np.concatenate([[0.0], np.cumsum(0.5 * np.log((2.0 * ladder + 1.0) / (2.0 * ladder)))])
    return np.repeat((0.5 * np.log(0.5) + gains)[:, None], total_lat, axis=1).astype(np.float32)


def order_columns(counts_ref, order_ref, ranks, batch_rows):
    lon_local, lat_local = counts_ref.shape
    groups, batch = order_ref.shape[1:]
    narrow = jnp.bfloat16

    def product(a, b):
        return jnp.dot(a, b.astype(narrow), preferred_element_type=jnp.float32)

    counts = counts_ref[...]
    at_row = lax.broadcasted_iota(jnp.int32, (lat_local, lat_local), 0)
    at_col = lax.broadcasted_iota(jnp.int32, (lat_local, lat_local), 1)
    before = (at_row < at_col).astype(jnp.float32)
    every = jnp.ones((lat_local, lat_local), jnp.float32)
    row = lax.broadcasted_iota(jnp.int32, (lon_local, lon_local), 0)
    col = lax.broadcasted_iota(jnp.int32, (lon_local, lon_local), 1)
    same = row // batch_rows == col // batch_rows
    above = (same & (col < row)).astype(jnp.float32).astype(narrow)
    block = same.astype(jnp.float32).astype(narrow)
    rank = jnp.zeros((lon_local, lat_local), jnp.float32)
    fewer = jnp.zeros((lon_local, lat_local), jnp.float32)
    for value in range(1, 9):
        member = (counts == value).astype(jnp.float32)
        in_row = product(member.astype(narrow), before)
        row_sums = product(member.astype(narrow), every)
        rank = rank + member * (fewer + in_row + product(above, row_sums))
        fewer = fewer + product(block, row_sums)
    ranks[...] = rank.astype(jnp.int32)

    spot = lax.broadcasted_iota(jnp.int32, (groups, lat_local), 0)
    slot = lax.broadcasted_iota(jnp.int32, (batch, lat_local), 0)
    lats = lax.broadcasted_iota(jnp.int32, (batch, lat_local), 1)

    def invert(chunk, carry):
        columns = jnp.zeros((groups, batch), jnp.float32)
        amounts = jnp.zeros((groups, batch), jnp.float32)
        for at in range(batch_rows):
            line = pl.ds(chunk * batch_rows + at, 1)
            mine = ranks[line, :]
            high = (spot == mine // batch).astype(jnp.float32).astype(narrow)
            low = slot == mine % batch
            column = jnp.where(low, lats + at * lat_local, 0).astype(jnp.float32).astype(narrow)
            amount = jnp.where(low, counts_ref[line, :], 0).astype(jnp.float32).astype(narrow)
            dims = (((1,), (1,)), ((), ()))
            columns += lax.dot_general(high, column, dims, preferred_element_type=jnp.float32)
            amounts += lax.dot_general(high, amount, dims, preferred_element_type=jnp.float32)
        order_ref[chunk] = (columns + 256.0 * amounts).astype(jnp.int32)
        return carry

    lax.fori_loop(0, order_ref.shape[0], invert, 0)


def spectral_kernel(
    lon_devices, lat_devices, modes, chunks, batch_rows,
    trunc_ref, state_ref, forward_ref, back_ref, lat_ref, counts_ref, out_ref, order_ref,
    theta, table, heat, ranks, forward, back, send1, recv1, send2, recv2,
    load_sem, table_sem, s1_sem, r1_sem, s2_sem, r2_sem,
):
    grp = lax.axis_index("grp")
    lon = lax.axis_index("lon")
    lat = lax.axis_index("lat")
    peers = lon_devices * lat_devices
    per_peer = modes // peers
    me = lon * lat_devices + lat
    lon_local, lat_local, cells = theta.shape
    rows = lon_local // chunks

    def theta_copy(chunk):
        span = pl.ds(chunk * rows, rows)
        return pltpu.make_async_copy(state_ref.at[0, span], theta.at[span], load_sem.at[chunk])

    for chunk in range(chunks):
        theta_copy(chunk).start()
    forward_copy = pltpu.make_async_copy(forward_ref.at[lon], forward, table_sem.at[0])
    back_copy = pltpu.make_async_copy(back_ref.at[lon], back, table_sem.at[1])
    forward_copy.start()
    back_copy.start()

    barrier = pltpu.get_barrier_semaphore()

    def place(offset):
        peer = lax.rem(me + offset, peers)
        return peer, (grp, peer // lat_devices, lax.rem(peer, lat_devices))

    def greet(offset, carry):
        _, device = place(offset)
        pl.semaphore_signal(barrier, inc=1, device_id=device, device_id_type=MESH)
        return carry

    lax.fori_loop(1, peers, greet, 0)

    total_lat = table.shape[1]
    sin_lat = lat_ref[0:8]
    weight = lat_ref[8:16]
    order_f = (me * per_peer + lax.broadcasted_iota(jnp.int32, (8, total_lat), 0)).astype(jnp.float32)
    start = jnp.concatenate(
        [lat_ref[pl.ds(24 + me * per_peer + at, 1), :] for at in range(8)], axis=0
    )
    diagonal = jnp.exp(start + order_f * lat_ref[16:24])
    zero = jnp.zeros((8, total_lat), jnp.float32)

    def rung(degree_f, carry):
        previous, earlier, inverse = carry
        higher = degree_f > order_f
        numerator = jnp.maximum(4.0 * degree_f * degree_f - 1.0, 1.0)
        denominator = jnp.where(higher, degree_f * degree_f - order_f * order_f, 1.0)
        mixed = lax.rsqrt(numerator * denominator)
        factor = numerator * mixed
        back_factor = denominator * mixed
        raised = factor * (sin_lat * previous - inverse * earlier)
        current = jnp.where(degree_f == order_f, diagonal, jnp.where(higher, raised, 0.0))
        return current, previous, jnp.where(higher, back_factor, 0.0)

    def ladder(block, carry):
        for at in range(8):
            degree = block * 8 + at
            carry = rung(degree.astype(jnp.float32), carry)
            table[pl.ds(pl.multiple_of(degree * 8, 8), 8), :] = carry[0]
        return carry

    lax.fori_loop(0, NN // 8, ladder, (zero, zero, zero))

    ones = jnp.ones((8, 128), jnp.float32)
    for chunk in range(chunks):
        theta_copy(chunk).wait()
        totals = []
        for at in range(rows):
            row = chunk * rows + at
            total = theta[row, :, 0:128]
            for tile in range(1, cells // 128):
                total = total + theta[row, :, tile * 128:(tile + 1) * 128]
            totals.append(total)
        sums = lax.dot_general(
            ones, jnp.concatenate(totals, axis=0), (((1,), (1,)), ((), ())),
            precision=HIGHEST, preferred_element_type=jnp.float32,
        )
        for at in range(rows):
            row = chunk * rows + at
            heat[row:row + 1, :] = sums[0:1, at * lat_local:(at + 1) * lat_local]
    forward_copy.wait()
    back_copy.wait()
    heating = heat[...]
    coefs = jnp.dot(forward[...], heating, precision=HIGHEST, preferred_element_type=jnp.float32)
    send1[...] = coefs.reshape(peers, 16, lat_local)
    pl.semaphore_wait(barrier, peers - 1)

    def first(offset):
        peer, device = place(offset)
        return pltpu.make_async_remote_copy(
            src_ref=send1.at[peer], dst_ref=recv1.at[me],
            send_sem=s1_sem.at[peer], recv_sem=r1_sem.at[me],
            device_id=device, device_id_type=MESH,
        )

    def first_arrival(offset):
        peer, device = place(offset)
        return pltpu.make_async_remote_copy(
            src_ref=send1.at[peer], dst_ref=recv1.at[peer],
            send_sem=s1_sem.at[peer], recv_sem=r1_sem.at[peer],
            device_id=device, device_id_type=MESH,
        )

    def second(offset):
        peer, device = place(offset)
        return pltpu.make_async_remote_copy(
            src_ref=send2.at[lax.rem(peer, lat_devices)], dst_ref=recv2.at[me],
            send_sem=s2_sem.at[peer], recv_sem=r2_sem.at[me],
            device_id=device, device_id_type=MESH,
        )

    def second_arrival(offset):
        peer, device = place(offset)
        return pltpu.make_async_remote_copy(
            src_ref=send2.at[lax.rem(peer, lat_devices)], dst_ref=recv2.at[peer],
            send_sem=s2_sem.at[peer], recv_sem=r2_sem.at[peer],
            device_id=device, device_id_type=MESH,
        )

    def for_peers(act):
        def step(offset, carry):
            act(offset)
            return carry
        lax.fori_loop(1, peers, step, 0)

    for_peers(lambda offset: first(offset).start())
    recv1[me] = send1[me]
    order_columns(counts_ref, order_ref, ranks, batch_rows)
    for_peers(lambda offset: first_arrival(offset).wait_recv())
    halves = []
    for half in range(lat_devices):
        total = recv1[half]
        for at in range(1, lon_devices):
            total = total + recv1[at * lat_devices + half]
        halves.append(total)
    whole = jnp.concatenate(halves, axis=1)
    weighted = whole * jnp.concatenate([weight, weight], axis=0)

    width = table.shape[0]
    spectrum = lax.dot_general(
        weighted, table[...], (((1,), (1,)), ((), ())),
        precision=HIGHEST, preferred_element_type=jnp.float32,
    )
    lane = lax.broadcasted_iota(jnp.int32, (16, width), 1)
    own = lax.rem(lax.broadcasted_iota(jnp.int32, (16, width), 0), 8)
    kept = jnp.full((16, width), -1, jnp.int32)
    for at in range(per_peer):
        kept = jnp.where(own == at, trunc_ref[me * per_peer + at], kept)
    keep = (lane % 8 == own) & (lane // 8 <= kept)
    filtered = jnp.dot(
        jnp.where(keep, spectrum, 0.0), table[...],
        precision=HIGHEST, preferred_element_type=jnp.float32,
    )
    for half in range(lat_devices):
        send2[half] = filtered[:, half * lat_local:(half + 1) * lat_local]
    for_peers(lambda offset: second(offset).start())
    recv2[me] = send2[lat]
    for_peers(lambda offset: second_arrival(offset).wait_recv())
    gathered = recv2[...].reshape(peers * 16, lat_local)
    out_ref[...] = jnp.dot(
        back[...], gathered, precision=HIGHEST, preferred_element_type=jnp.float32
    )
    for_peers(lambda offset: first(offset).wait_send())
    for_peers(lambda offset: second(offset).wait_send())


def spectral_forcing(cloud_state, counts, truncation, batch_rows):
    lon_devices = lax.axis_size("lon")
    lat_devices = lax.axis_size("lat")
    peers = lon_devices * lat_devices
    _, lon_local, lat_local, cells = cloud_state.shape
    total_lon, total_lat = lon_local * lon_devices, lat_local * lat_devices
    modes = truncation.shape[0]
    chunks = 8 if lon_local % 8 == 0 else 1
    forward, back = wave_tables(total_lon, lon_devices, modes, peers, 1.0 / (total_lon * cells))
    lat_consts = np.concatenate(
        [latitude_rows(total_lat).reshape(24, total_lat), order_starts(modes, total_lat)]
    )
    groups = batch_rows * lat_local // BATCH
    vmem = pl.BlockSpec(memory_space=pltpu.VMEM)
    hbm = pl.BlockSpec(memory_space=pl.ANY)
    return pl.pallas_call(
        functools.partial(spectral_kernel, lon_devices, lat_devices, modes, chunks, batch_rows),
        out_shape=(
            jax.ShapeDtypeStruct((lon_local, lat_local), jnp.float32),
            jax.ShapeDtypeStruct((lon_local // batch_rows, groups, BATCH), jnp.int32),
        ),
        in_specs=[pl.BlockSpec(memory_space=pltpu.SMEM), hbm, hbm, hbm, vmem, vmem],
        out_specs=(vmem, vmem),
        scratch_shapes=[
            pltpu.VMEM((lon_local, lat_local, cells), jnp.float32),
            pltpu.VMEM((NN * 8, total_lat), jnp.float32),
            pltpu.VMEM((lon_local, lat_local), jnp.float32),
            pltpu.VMEM((lon_local, lat_local), jnp.int32),
            pltpu.VMEM(forward.shape[1:], jnp.float32),
            pltpu.VMEM(back.shape[1:], jnp.float32),
            pltpu.VMEM((peers, 16, lat_local), jnp.float32),
            pltpu.VMEM((peers, 16, lat_local), jnp.float32),
            pltpu.VMEM((lat_devices, 16, lat_local), jnp.float32),
            pltpu.VMEM((peers, 16, lat_local), jnp.float32),
            pltpu.SemaphoreType.DMA((chunks,)),
            pltpu.SemaphoreType.DMA((2,)),
            pltpu.SemaphoreType.DMA((peers,)),
            pltpu.SemaphoreType.DMA((peers,)),
            pltpu.SemaphoreType.DMA((peers,)),
            pltpu.SemaphoreType.DMA((peers,)),
        ],
        compiler_params=pltpu.CompilerParams(
            collective_id=0, has_side_effects=True, vmem_limit_bytes=60 << 20
        ),
        name="spectral",
    )(truncation, cloud_state, jnp.asarray(forward), jnp.asarray(back), jnp.asarray(lat_consts), counts)


BATCH = 16


def swap_blocks(cols, low_half, even):
    a0 = jnp.where(low_half, cols[0], pltpu.roll(cols[2], 64, 1))
    b0 = jnp.where(low_half, pltpu.roll(cols[0], 64, 1), cols[2])
    a1 = jnp.where(low_half, cols[1], pltpu.roll(cols[3], 64, 1))
    b1 = jnp.where(low_half, pltpu.roll(cols[1], 64, 1), cols[3])
    return [
        jnp.where(even, a0, pltpu.roll(a1, 32, 1)),
        jnp.where(even, pltpu.roll(a0, 96, 1), a1),
        jnp.where(even, b0, pltpu.roll(b1, 32, 1)),
        jnp.where(even, pltpu.roll(b0, 96, 1), b1),
    ]


def cloud_kernel(lat_local, order_ref, force_ref, const_ref, x_ref, o_ref):
    chunk = pl.program_id(0)
    blocks = x_ref.shape[1]
    rows = blocks * 8 // lat_local
    lane = lax.broadcasted_iota(jnp.int32, (8, 128), 1)
    low_half = lane < 64
    even = (lane // 32) % 2 == 0
    kappa = 0.275 / 0.725
    lat_bits = lat_local.bit_length() - 1

    def batch(index, carry):
        entries = [order_ref[chunk, index, at] for at in range(BATCH)]
        spots = [((entry & 255) >> 3, entry & 7) for entry in entries]
        counts = [entry >> 8 for entry in entries]
        forces = [
            force_ref[chunk * rows + ((entry & 255) >> lat_bits), entry & (lat_local - 1)]
            for entry in entries
        ]
        rho = const_ref[0]
        profile = const_ref[1]
        us, ws, heats, trips = [], [], [], []
        for group in range(BATCH // 4):
            u4, w4 = [], []
            for at in range(group * 4, group * 4 + 4):
                block, sub = spots[at][0], spots[at][1]
                theta = x_ref[0, block, pl.ds(sub, 8, stride=8), :]
                moist = x_ref[1, block, pl.ds(sub, 8, stride=8), :]
                u4.append((10.0 / 0.725) * moist - (2.0 / 0.725) * theta - (10.0 / 0.725))
                w4.append(theta + 0.5 * moist)
            us += swap_blocks(u4, low_half, even)
            ws += swap_blocks(w4, low_half, even)

            def spread(values):
                first = jnp.where(even, values[0], values[1])
                second = jnp.where(even, values[2], values[3])
                return jnp.where(low_half, first, second)

            heats.append(spread(forces[group * 4:group * 4 + 4]) * profile)
            trips.append(spread(counts[group * 4:group * 4 + 4]))

        def advance(masked, step, state):
            us, ws = state
            scale = const_ref[2 + 9 + step + 1]
            floor = scale * scale
            next_us, next_ws = [], []
            for group in range(BATCH // 4):
                active = step < trips[group]
                push = 2.0 * heats[group] * scale
                u4 = us[group * 4:group * 4 + 4]
                w4 = ws[group * 4:group * 4 + 4]
                u_before = [pltpu.roll(u4[3], 1, 0)] + list(u4[:3])
                w_before = [pltpu.roll(w4[3], 1, 0)] + list(w4[:3])
                for at in range(4):
                    y = u4[at] + rho * u_before[at] - push
                    z = y * y + floor
                    root = z * lax.rsqrt(z)
                    next_us.append(y - kappa * root)
                    next_ws.append(w4[at] + rho * w_before[at])
                    if masked:
                        next_us[-1] = jnp.where(active, next_us[-1], u4[at])
                        next_ws[-1] = jnp.where(active, next_ws[-1], w4[at])
            return tuple(next_us), tuple(next_ws)

        state = (tuple(us), tuple(ws))
        state = lax.fori_loop(0, counts[0], functools.partial(advance, False), state)
        us, ws = lax.fori_loop(counts[0], counts[-1], functools.partial(advance, True), state)

        for group in range(BATCH // 4):
            def spread_rows(base):
                rows4 = [const_ref[base + counts[group * 4 + at]] for at in range(4)]
                return jnp.where(
                    low_half, jnp.where(even, rows4[0], rows4[1]), jnp.where(even, rows4[2], rows4[3])
                )

            u_scale = spread_rows(2 + 18)
            w_scale = spread_rows(2)
            shift = trips[group].astype(jnp.float32) * heats[group] * (1.0 / 1.1) - 0.5 / 1.1
            u_theta = u_scale * (0.5 / 1.1)
            thetas, moists = [], []
            for at in range(4):
                u, w = us[group * 4 + at], ws[group * 4 + at]
                theta = w_scale * w - u_theta * u + shift
                thetas.append(theta)
                moists.append(u_scale * u + (1.0 + 0.2 * theta))
            thetas = swap_blocks(thetas, low_half, even)
            moists = swap_blocks(moists, low_half, even)
            for at in range(4):
                block, sub = spots[group * 4 + at][0], spots[group * 4 + at][1]
                o_ref[0, block, pl.ds(sub, 8, stride=8), :] = thetas[at]
                o_ref[1, block, pl.ds(sub, 8, stride=8), :] = moists[at]
        return carry

    lax.fori_loop(0, blocks * 8 // BATCH, batch, 0)


def cloud_constants(courant, levels):
    rate = jnp.tile(courant, 128 // levels)
    level = jnp.tile(jnp.sin(jnp.pi * (jnp.arange(levels).astype(jnp.float32) + 0.5) / levels), 128 // levels)
    keep = 1.0 - rate
    lower = 0.725 * keep
    inverse = 1.0 / lower

    def powers(base, first):
        out = [first]
        for _ in range(8):
            out.append(out[-1] * base)
        return out

    one = jnp.ones_like(rate)
    rows = [rate / keep, COUPLE * level]
    rows += powers(keep, one / 1.1) + powers(inverse, one) + powers(lower, one * 0.0725)
    return jnp.broadcast_to(jnp.stack(rows)[:, None, :], (len(rows), 8, 128))


def shards(cloud_state, counts, courant, truncation):
    fields, lon_local, lat_local, cells = cloud_state.shape
    levels = courant.shape[0]
    rows = min(256 // lat_local, lon_local)
    forcing, order = spectral_forcing(cloud_state, counts, truncation, rows)
    consts = cloud_constants(courant, levels)
    lat_blocks, tiles = lat_local // 8, cells // 128
    view = cloud_state.reshape(fields, lon_local, lat_blocks, 8, tiles, 128)
    view = view.transpose(0, 1, 2, 4, 3, 5).reshape(fields, lon_local * lat_blocks, tiles * 8, 128)
    block = pl.BlockSpec((fields, rows * lat_blocks, tiles * 8, 128), lambda i: (0, i, 0, 0))
    smem = pl.BlockSpec(memory_space=pltpu.SMEM)
    updated = pl.pallas_call(
        functools.partial(cloud_kernel, lat_local),
        out_shape=jax.ShapeDtypeStruct(view.shape, jnp.float32),
        grid=(lon_local // rows,),
        in_specs=[smem, smem, pl.BlockSpec(memory_space=pltpu.VMEM), block],
        out_specs=block,
        compiler_params=pltpu.CompilerParams(vmem_limit_bytes=60 << 20),
        name="cloud",
    )(order, forcing, consts, view)
    updated = updated.reshape(fields, lon_local, lat_blocks, tiles, 8, 128).transpose(0, 1, 2, 4, 3, 5)
    return updated.reshape(cloud_state.shape)


def solution(mesh):
    return jax.shard_map(
        shards,
        mesh=mesh,
        in_specs=(P("grp", "lon", "lat", None), P(("grp", "lon"), "lat"), P(), P()),
        out_specs=P("grp", "lon", "lat", None),
        check_vma=False,
    )
```

```python
import functools

import jax
import jax.numpy as jnp
import numpy as np
from jax import lax
from jax.experimental import pallas as pl
from jax.experimental.pallas import tpu as pltpu
from jax.sharding import PartitionSpec as P

NN = 96
COUPLE = 8.0
HIGHEST = lax.Precision.HIGHEST
MESH = pl.DeviceIdType.MESH


def wave_tables(total_lon, lon_devices, modes, peers, scale):
    per_peer = modes // peers
    lon_local = total_lon // lon_devices
    rows = np.zeros((peers, 2, 8, total_lon))
    back = np.zeros((peers, 2, 8, total_lon))
    lons = np.arange(total_lon)
    for peer in range(peers):
        for at in range(per_peer):
            mode = peer * per_peer + at
            angle = 2.0 * np.pi * ((lons * mode) % total_lon) / total_lon
            rows[peer, 0, at], rows[peer, 1, at] = np.cos(angle), np.sin(angle)
            back[peer, :, at] = rows[peer, :, at] * (1.0 if mode == 0 else 2.0)
    rows = rows.reshape(peers * 16, lon_devices, lon_local).transpose(1, 0, 2) * scale
    back = back.reshape(peers * 16, lon_devices, lon_local).transpose(1, 2, 0)
    return rows.astype(np.float32), back.astype(np.float32)


def latitude_rows(total_lat):
    latitude = -0.5 * np.pi + np.pi * (np.arange(total_lat) + 0.5) / total_lat
    cosine = np.cos(latitude)
    rows = np.stack([np.sin(latitude), np.pi * cosine / total_lat, np.log(cosine)])
    return np.repeat(rows[:, None, :], 8, axis=1).astype(np.float32)


def order_starts(modes, total_lat):
    ladder = np.arange(1, modes + 8)
    gains = np.concatenate([[0.0], np.cumsum(0.5 * np.log((2.0 * ladder + 1.0) / (2.0 * ladder)))])
    return np.repeat((0.5 * np.log(0.5) + gains)[:, None], total_lat, axis=1).astype(np.float32)


def spread_columns(values, levels, precision):
    lon_local = values.shape[0]
    shape = (lon_local, lon_local * levels)
    own = lax.broadcasted_iota(jnp.int32, shape, 1) // levels == lax.broadcasted_iota(jnp.int32, shape, 0)
    return lax.dot_general(
        values, own.astype(jnp.float32), (((0,), (0,)), ((), ())),
        precision=precision, preferred_element_type=jnp.float32,
    )


def count_bounds(counts_ref, least_ref, most_ref, group):
    lon_local, lat_local = counts_ref.shape
    narrow = jnp.bfloat16
    counts = counts_ref[...]

    def same(extent, size):
        row = lax.broadcasted_iota(jnp.int32, (extent, extent), 0)
        col = lax.broadcasted_iota(jnp.int32, (extent, extent), 1)
        return (row // size == col // size).astype(jnp.float32).astype(narrow)

    lons, lats = same(lon_local, group), same(lat_local, 8)
    least = jnp.zeros((lon_local, lat_local), jnp.int32)
    most = jnp.zeros((lon_local, lat_local), jnp.int32)
    for value in range(1, 9):
        member = (counts >= value).astype(jnp.float32).astype(narrow)
        across = jnp.dot(member, lats, preferred_element_type=jnp.float32)
        total = jnp.dot(lons, across.astype(narrow), preferred_element_type=jnp.float32)
        least = least + (total > group * 8 - 0.5).astype(jnp.int32)
        most = most + (total > 0.5).astype(jnp.int32)
    least_ref[...] = least
    most_ref[...] = most


def spectral_kernel(
    lon_devices, lat_devices, modes, chunks, levels,
    trunc_ref, state_ref, forward_ref, back_ref, lat_ref, counts_ref, heat_ref, trips_ref, least_ref, most_ref,
    theta, table, heat, forward, back, send1, recv1, send2, recv2,
    load_sem, table_sem, s1_sem, r1_sem, s2_sem, r2_sem,
):
    grp = lax.axis_index("grp")
    lon = lax.axis_index("lon")
    lat = lax.axis_index("lat")
    peers = lon_devices * lat_devices
    per_peer = modes // peers
    me = lon * lat_devices + lat
    lon_local, lat_local, cells = theta.shape
    rows = lon_local // chunks

    def theta_copy(chunk):
        span = pl.ds(chunk * rows, rows)
        return pltpu.make_async_copy(state_ref.at[0, span], theta.at[span], load_sem.at[chunk])

    for chunk in range(chunks):
        theta_copy(chunk).start()
    forward_copy = pltpu.make_async_copy(forward_ref.at[lon], forward, table_sem.at[0])
    back_copy = pltpu.make_async_copy(back_ref.at[lon], back, table_sem.at[1])
    forward_copy.start()
    back_copy.start()

    barrier = pltpu.get_barrier_semaphore()

    def place(offset):
        peer = lax.rem(me + offset, peers)
        return peer, (grp, peer // lat_devices, lax.rem(peer, lat_devices))

    def greet(offset, carry):
        _, device = place(offset)
        pl.semaphore_signal(barrier, inc=1, device_id=device, device_id_type=MESH)
        return carry

    lax.fori_loop(1, peers, greet, 0)

    total_lat = table.shape[1]
    sin_lat = lat_ref[0:8]
    weight = lat_ref[8:16]
    order_f = (me * per_peer + lax.broadcasted_iota(jnp.int32, (8, total_lat), 0)).astype(jnp.float32)
    start = jnp.concatenate(
        [lat_ref[pl.ds(24 + me * per_peer + at, 1), :] for at in range(8)], axis=0
    )
    diagonal = jnp.exp(start + order_f * lat_ref[16:24])
    zero = jnp.zeros((8, total_lat), jnp.float32)

    def rung(degree_f, carry):
        previous, earlier, inverse = carry
        higher = degree_f > order_f
        numerator = jnp.maximum(4.0 * degree_f * degree_f - 1.0, 1.0)
        denominator = jnp.where(higher, degree_f * degree_f - order_f * order_f, 1.0)
        mixed = lax.rsqrt(numerator * denominator)
        factor = numerator * mixed
        back_factor = denominator * mixed
        raised = factor * (sin_lat * previous - inverse * earlier)
        current = jnp.where(degree_f == order_f, diagonal, jnp.where(higher, raised, 0.0))
        return current, previous, jnp.where(higher, back_factor, 0.0)

    def ladder(block, carry):
        for at in range(8):
            degree = block * 8 + at
            carry = rung(degree.astype(jnp.float32), carry)
            table[pl.ds(pl.multiple_of(degree * 8, 8), 8), :] = carry[0]
        return carry

    lax.fori_loop(0, NN // 8, ladder, (zero, zero, zero))

    ones = jnp.ones((8, 128), jnp.float32)
    for chunk in range(chunks):
        theta_copy(chunk).wait()
        totals = []
        for at in range(rows):
            row = chunk * rows + at
            total = theta[row, :, 0:128]
            for tile in range(1, cells // 128):
                total = total + theta[row, :, tile * 128:(tile + 1) * 128]
            totals.append(total)
        sums = lax.dot_general(
            ones, jnp.concatenate(totals, axis=0), (((1,), (1,)), ((), ())),
            precision=HIGHEST, preferred_element_type=jnp.float32,
        )
        for at in range(rows):
            row = chunk * rows + at
            heat[row:row + 1, :] = sums[0:1, at * lat_local:(at + 1) * lat_local]
    forward_copy.wait()
    back_copy.wait()
    heating = heat[...]
    coefs = jnp.dot(forward[...], heating, precision=HIGHEST, preferred_element_type=jnp.float32)
    send1[...] = coefs.reshape(peers, 16, lat_local)
    pl.semaphore_wait(barrier, peers - 1)

    def first(offset):
        peer, device = place(offset)
        return pltpu.make_async_remote_copy(
            src_ref=send1.at[peer], dst_ref=recv1.at[me],
            send_sem=s1_sem.at[peer], recv_sem=r1_sem.at[me],
            device_id=device, device_id_type=MESH,
        )

    def first_arrival(offset):
        peer, device = place(offset)
        return pltpu.make_async_remote_copy(
            src_ref=send1.at[peer], dst_ref=recv1.at[peer],
            send_sem=s1_sem.at[peer], recv_sem=r1_sem.at[peer],
            device_id=device, device_id_type=MESH,
        )

    def second(offset):
        peer, device = place(offset)
        return pltpu.make_async_remote_copy(
            src_ref=send2.at[lax.rem(peer, lat_devices)], dst_ref=recv2.at[me],
            send_sem=s2_sem.at[peer], recv_sem=r2_sem.at[me],
            device_id=device, device_id_type=MESH,
        )

    def second_arrival(offset):
        peer, device = place(offset)
        return pltpu.make_async_remote_copy(
            src_ref=send2.at[lax.rem(peer, lat_devices)], dst_ref=recv2.at[peer],
            send_sem=s2_sem.at[peer], recv_sem=r2_sem.at[peer],
            device_id=device, device_id_type=MESH,
        )

    def for_peers(act):
        def step(offset, carry):
            act(offset)
            return carry
        lax.fori_loop(1, peers, step, 0)

    for_peers(lambda offset: first(offset).start())
    recv1[me] = send1[me]
    count_bounds(counts_ref, least_ref, most_ref, 128 // levels)
    trips_ref[...] = spread_columns(counts_ref[...].astype(jnp.float32), levels, HIGHEST)
    for_peers(lambda offset: first_arrival(offset).wait_recv())
    halves = []
    for half in range(lat_devices):
        total = recv1[half]
        for at in range(1, lon_devices):
            total = total + recv1[at * lat_devices + half]
        halves.append(total)
    whole = jnp.concatenate(halves, axis=1)
    weighted = whole * jnp.concatenate([weight, weight], axis=0)

    width = table.shape[0]
    spectrum = lax.dot_general(
        weighted, table[...], (((1,), (1,)), ((), ())),
        precision=HIGHEST, preferred_element_type=jnp.float32,
    )
    lane = lax.broadcasted_iota(jnp.int32, (16, width), 1)
    own = lax.rem(lax.broadcasted_iota(jnp.int32, (16, width), 0), 8)
    kept = jnp.full((16, width), -1, jnp.int32)
    for at in range(per_peer):
        kept = jnp.where(own == at, trunc_ref[me * per_peer + at], kept)
    keep = (lane % 8 == own) & (lane // 8 <= kept)
    filtered = jnp.dot(
        jnp.where(keep, spectrum, 0.0), table[...],
        precision=HIGHEST, preferred_element_type=jnp.float32,
    )
    for half in range(lat_devices):
        send2[half] = filtered[:, half * lat_local:(half + 1) * lat_local]
    for_peers(lambda offset: second(offset).start())
    recv2[me] = send2[lat]
    for_peers(lambda offset: second_arrival(offset).wait_recv())
    gathered = recv2[...].reshape(peers * 16, lat_local)
    forcing = jnp.dot(
        back[...], gathered, precision=HIGHEST, preferred_element_type=jnp.float32
    )
    heat_ref[...] = spread_columns(forcing, levels, HIGHEST)
    for_peers(lambda offset: first(offset).wait_send())
    for_peers(lambda offset: second(offset).wait_send())


def spectral_forcing(cloud_state, counts, truncation, levels):
    lon_devices = lax.axis_size("lon")
    lat_devices = lax.axis_size("lat")
    peers = lon_devices * lat_devices
    _, lon_local, lat_local, cells = cloud_state.shape
    total_lon, total_lat = lon_local * lon_devices, lat_local * lat_devices
    modes = truncation.shape[0]
    chunks = 8 if lon_local % 8 == 0 else 1
    forward, back = wave_tables(total_lon, lon_devices, modes, peers, 1.0 / (total_lon * cells))
    lat_consts = np.concatenate(
        [latitude_rows(total_lat).reshape(24, total_lat), order_starts(modes, total_lat)]
    )
    vmem = pl.BlockSpec(memory_space=pltpu.VMEM)
    hbm = pl.BlockSpec(memory_space=pl.ANY)
    return pl.pallas_call(
        functools.partial(spectral_kernel, lon_devices, lat_devices, modes, chunks, levels),
        out_shape=(
            jax.ShapeDtypeStruct((lat_local, lon_local * levels), jnp.float32),
            jax.ShapeDtypeStruct((lat_local, lon_local * levels), jnp.float32),
            jax.ShapeDtypeStruct((lon_local, lat_local), jnp.int32),
            jax.ShapeDtypeStruct((lon_local, lat_local), jnp.int32),
        ),
        in_specs=[pl.BlockSpec(memory_space=pltpu.SMEM), hbm, hbm, hbm, vmem, vmem],
        out_specs=(vmem,) * 4,
        scratch_shapes=[
            pltpu.VMEM((lon_local, lat_local, cells), jnp.float32),
            pltpu.VMEM((NN * 8, total_lat), jnp.float32),
            pltpu.VMEM((lon_local, lat_local), jnp.float32),
            pltpu.VMEM(forward.shape[1:], jnp.float32),
            pltpu.VMEM(back.shape[1:], jnp.float32),
            pltpu.VMEM((peers, 16, lat_local), jnp.float32),
            pltpu.VMEM((peers, 16, lat_local), jnp.float32),
            pltpu.VMEM((lat_devices, 16, lat_local), jnp.float32),
            pltpu.VMEM((peers, 16, lat_local), jnp.float32),
            pltpu.SemaphoreType.DMA((chunks,)),
            pltpu.SemaphoreType.DMA((2,)),
            pltpu.SemaphoreType.DMA((peers,)),
            pltpu.SemaphoreType.DMA((peers,)),
            pltpu.SemaphoreType.DMA((peers,)),
            pltpu.SemaphoreType.DMA((peers,)),
        ],
        compiler_params=pltpu.CompilerParams(
            collective_id=0, has_side_effects=True, vmem_limit_bytes=60 << 20
        ),
        name="spectral",
    )(truncation, cloud_state, jnp.asarray(forward), jnp.asarray(back), jnp.asarray(lat_consts), counts)


def swap_blocks(cols, low_half, even):
    a0 = jnp.where(low_half, cols[0], pltpu.roll(cols[2], 64, 1))
    b0 = jnp.where(low_half, pltpu.roll(cols[0], 64, 1), cols[2])
    a1 = jnp.where(low_half, cols[1], pltpu.roll(cols[3], 64, 1))
    b1 = jnp.where(low_half, pltpu.roll(cols[1], 64, 1), cols[3])
    return [
        jnp.where(even, a0, pltpu.roll(a1, 32, 1)),
        jnp.where(even, pltpu.roll(a0, 96, 1), a1),
        jnp.where(even, b0, pltpu.roll(b1, 32, 1)),
        jnp.where(even, pltpu.roll(b0, 96, 1), b1),
    ]


def cloud_kernel(
    lat_blocks, least_ref, most_ref, const_ref, heat_ref, trips_ref, x_ref, o_ref, u_ref, w_ref
):
    chunk = pl.program_id(0)
    group = x_ref.shape[1] // lat_blocks
    tiles = x_ref.shape[2] // 8
    cells = tiles * group
    lane = lax.broadcasted_iota(jnp.int32, (8, 128), 1)
    low_half = lane < 64
    even = (lane // 32) % 2 == 0
    kappa = 0.275 / 0.725

    def batch(jb, carry):
        least = least_ref[chunk * group, jb * 8]
        most = most_ref[chunk * group, jb * 8]
        lats = pl.ds(pl.multiple_of(jb * 8, 8), 8)
        heat = heat_ref[lats, :] * const_ref[1]
        trips = trips_ref[lats, :].astype(jnp.int32)
        rho = const_ref[0]
        us = []
        for tile in range(tiles):
            u4, w4 = [], []
            for at in range(group):
                theta = x_ref[0, at * lat_blocks + jb, tile * 8:tile * 8 + 8, :]
                moist = x_ref[1, at * lat_blocks + jb, tile * 8:tile * 8 + 8, :]
                u4.append((10.0 / 0.725) * moist - (2.0 / 0.725) * theta - (10.0 / 0.725))
                w4.append(theta + 0.5 * moist)
            us += swap_blocks(u4, low_half, even)
            for at, value in enumerate(swap_blocks(w4, low_half, even)):
                w_ref[tile * group + at] = value

        def advance_u(masked, step, us):
            scale = const_ref[2 + 9 + step + 1]
            floor = scale * scale
            push = 2.0 * heat * scale
            active = step < trips
            out = []
            for at in range(cells):
                y = us[at] + rho * us[at - 1] - push
                z = y * y + floor
                value = y - kappa * (z * lax.rsqrt(z))
                out.append(jnp.where(active, value, us[at]) if masked else value)
            return tuple(out)

        def advance_w(masked, step, ws):
            active = step < trips
            out = []
            for at in range(cells):
                value = ws[at] + rho * ws[at - 1]
                out.append(jnp.where(active, value, ws[at]) if masked else value)
            return tuple(out)

        us = lax.fori_loop(0, least, functools.partial(advance_u, False), tuple(us))
        us = lax.fori_loop(least, most, functools.partial(advance_u, True), us)
        for at in range(cells):
            u_ref[at] = us[at]
        ws = tuple(w_ref[at] for at in range(cells))
        ws = lax.fori_loop(0, least, functools.partial(advance_w, False), ws)
        ws = lax.fori_loop(least, most, functools.partial(advance_w, True), ws)

        u_scale = const_ref[2 + 18 + 1]
        w_scale = const_ref[2 + 1]
        for count in range(2, 9):
            u_scale = jnp.where(trips == count, const_ref[2 + 18 + count], u_scale)
            w_scale = jnp.where(trips == count, const_ref[2 + count], w_scale)
        shift = trips.astype(jnp.float32) * heat * (1.0 / 1.1) - 0.5 / 1.1
        u_theta = u_scale * (0.5 / 1.1)
        for tile in range(tiles):
            thetas, moists = [], []
            for at in range(group):
                u, w = u_ref[tile * group + at], ws[tile * group + at]
                theta = w_scale * w - u_theta * u + shift
                thetas.append(theta)
                moists.append(u_scale * u + (1.0 + 0.2 * theta))
            thetas = swap_blocks(thetas, low_half, even)
            moists = swap_blocks(moists, low_half, even)
            for at in range(group):
                o_ref[0, at * lat_blocks + jb, tile * 8:tile * 8 + 8, :] = thetas[at]
                o_ref[1, at * lat_blocks + jb, tile * 8:tile * 8 + 8, :] = moists[at]
        return carry

    lax.fori_loop(0, lat_blocks, batch, 0)


def cloud_constants(courant, levels):
    rate = jnp.tile(courant, 128 // levels)
    level = jnp.tile(jnp.sin(jnp.pi * (jnp.arange(levels).astype(jnp.float32) + 0.5) / levels), 128 // levels)
    keep = 1.0 - rate
    lower = 0.725 * keep
    inverse = 1.0 / lower

    def powers(base, first):
        out = [first]
        for _ in range(8):
            out.append(out[-1] * base)
        return out

    one = jnp.ones_like(rate)
    rows = [rate / keep, COUPLE * level]
    rows += powers(keep, one / 1.1) + powers(inverse, one) + powers(lower, one * 0.0725)
    return jnp.broadcast_to(jnp.stack(rows)[:, None, :], (len(rows), 8, 128))


def shards(cloud_state, counts, courant, truncation):
    fields, lon_local, lat_local, cells = cloud_state.shape
    levels = courant.shape[0]
    rows = 128 // levels
    heat, trips, least, most = spectral_forcing(cloud_state, counts, truncation, levels)
    consts = cloud_constants(courant, levels)
    lat_blocks, tiles = lat_local // 8, cells // 128
    view = cloud_state.reshape(fields, lon_local, lat_blocks, 8, tiles, 128)
    view = view.transpose(0, 1, 2, 4, 3, 5).reshape(fields, lon_local * lat_blocks, tiles * 8, 128)
    block = pl.BlockSpec((fields, rows * lat_blocks, tiles * 8, 128), lambda i: (0, i, 0, 0))
    smem = pl.BlockSpec(memory_space=pltpu.SMEM)
    updated = pl.pallas_call(
        functools.partial(cloud_kernel, lat_blocks),
        out_shape=jax.ShapeDtypeStruct(view.shape, jnp.float32),
        grid=(lon_local // rows,),
        in_specs=[
            smem, smem, pl.BlockSpec(memory_space=pltpu.VMEM),
            pl.BlockSpec((lat_local, 128), lambda i: (0, i)),
            pl.BlockSpec((lat_local, 128), lambda i: (0, i)),
            block,
        ],
        out_specs=block,
        scratch_shapes=[pltpu.VMEM((cells // levels, 8, 128), jnp.float32)] * 2,
        compiler_params=pltpu.CompilerParams(vmem_limit_bytes=60 << 20),
        name="cloud",
    )(least, most, consts, heat, trips, view)
    updated = updated.reshape(fields, lon_local, lat_blocks, tiles, 8, 128).transpose(0, 1, 2, 4, 3, 5)
    return updated.reshape(cloud_state.shape)


def solution(mesh):
    return jax.shard_map(
        shards,
        mesh=mesh,
        in_specs=(P("grp", "lon", "lat", None), P(("grp", "lon"), "lat"), P(), P()),
        out_specs=P("grp", "lon", "lat", None),
        check_vma=False,
    )
```

```python
import functools

import jax
import jax.numpy as jnp
import numpy as np
from jax import lax
from jax.experimental import pallas as pl
from jax.experimental.pallas import tpu as pltpu
from jax.sharding import PartitionSpec as P

NN = 96
COUPLE = 8.0
HIGHEST = lax.Precision.HIGHEST
MESH = pl.DeviceIdType.MESH


def wave_tables(total_lon, lon_devices, modes, peers, scale):
    per_peer = modes // peers
    lon_local = total_lon // lon_devices
    rows = np.zeros((peers, 2, 8, total_lon))
    back = np.zeros((peers, 2, 8, total_lon))
    lons = np.arange(total_lon)
    for peer in range(peers):
        for at in range(per_peer):
            mode = peer * per_peer + at
            angle = 2.0 * np.pi * ((lons * mode) % total_lon) / total_lon
            rows[peer, 0, at], rows[peer, 1, at] = np.cos(angle), np.sin(angle)
            back[peer, :, at] = rows[peer, :, at] * (1.0 if mode == 0 else 2.0)
    rows = rows.reshape(peers * 16, lon_devices, lon_local).transpose(1, 0, 2) * scale
    back = back.reshape(peers * 16, lon_devices, lon_local).transpose(1, 2, 0)
    return rows.astype(np.float32), back.astype(np.float32)


def latitude_rows(total_lat):
    latitude = -0.5 * np.pi + np.pi * (np.arange(total_lat) + 0.5) / total_lat
    cosine = np.cos(latitude)
    rows = np.stack([np.sin(latitude), np.pi * cosine / total_lat, np.log(cosine)])
    return np.repeat(rows[:, None, :], 8, axis=1).astype(np.float32)


def order_starts(modes, total_lat):
    ladder = np.arange(1, modes + 8)
    gains = np.concatenate([[0.0], np.cumsum(0.5 * np.log((2.0 * ladder + 1.0) / (2.0 * ladder)))])
    return np.repeat((0.5 * np.log(0.5) + gains)[:, None], total_lat, axis=1).astype(np.float32)


def spread_columns(values, levels, precision):
    lon_local = values.shape[0]
    shape = (lon_local, lon_local * levels)
    own = lax.broadcasted_iota(jnp.int32, shape, 1) // levels == lax.broadcasted_iota(jnp.int32, shape, 0)
    return lax.dot_general(
        values, own.astype(jnp.float32), (((0,), (0,)), ((), ())),
        precision=precision, preferred_element_type=jnp.float32,
    )


def count_bounds(counts_ref, least_ref, most_ref, group):
    lon_local, lat_local = counts_ref.shape
    narrow = jnp.bfloat16
    counts = counts_ref[...]

    def same(extent, size):
        row = lax.broadcasted_iota(jnp.int32, (extent, extent), 0)
        col = lax.broadcasted_iota(jnp.int32, (extent, extent), 1)
        return (row // size == col // size).astype(jnp.float32).astype(narrow)

    lons, lats = same(lon_local, group), same(lat_local, 8)
    least = jnp.zeros((lon_local, lat_local), jnp.int32)
    most = jnp.zeros((lon_local, lat_local), jnp.int32)
    for value in range(1, 9):
        member = (counts >= value).astype(jnp.float32).astype(narrow)
        across = jnp.dot(member, lats, preferred_element_type=jnp.float32)
        total = jnp.dot(lons, across.astype(narrow), preferred_element_type=jnp.float32)
        least = least + (total > group * 8 - 0.5).astype(jnp.int32)
        most = most + (total > 0.5).astype(jnp.int32)
    least_ref[...] = least
    most_ref[...] = most


def spectral_kernel(
    lon_devices, lat_devices, modes, chunks, levels,
    trunc_ref, state_ref, forward_ref, back_ref, lat_ref, counts_ref, heat_ref, trips_ref, least_ref, most_ref,
    theta, table, heat, forward, back, send1, recv1, send2, recv2,
    load_sem, table_sem, s1_sem, r1_sem, s2_sem, r2_sem,
):
    grp = lax.axis_index("grp")
    lon = lax.axis_index("lon")
    lat = lax.axis_index("lat")
    peers = lon_devices * lat_devices
    per_peer = modes // peers
    me = lon * lat_devices + lat
    lon_local, lat_local, cells = theta.shape
    rows = lon_local // chunks

    def theta_copy(chunk):
        span = pl.ds(chunk * rows, rows)
        return pltpu.make_async_copy(state_ref.at[0, span], theta.at[span], load_sem.at[chunk])

    for chunk in range(chunks):
        theta_copy(chunk).start()
    forward_copy = pltpu.make_async_copy(forward_ref.at[lon], forward, table_sem.at[0])
    back_copy = pltpu.make_async_copy(back_ref.at[lon], back, table_sem.at[1])
    forward_copy.start()
    back_copy.start()

    barrier = pltpu.get_barrier_semaphore()

    def place(offset):
        peer = lax.rem(me + offset, peers)
        return peer, (grp, peer // lat_devices, lax.rem(peer, lat_devices))

    def greet(offset, carry):
        _, device = place(offset)
        pl.semaphore_signal(barrier, inc=1, device_id=device, device_id_type=MESH)
        return carry

    lax.fori_loop(1, peers, greet, 0)

    total_lat = table.shape[1]
    sin_lat = lat_ref[0:8]
    weight = lat_ref[8:16]
    order_f = (me * per_peer + lax.broadcasted_iota(jnp.int32, (8, total_lat), 0)).astype(jnp.float32)
    start = jnp.concatenate(
        [lat_ref[pl.ds(24 + me * per_peer + at, 1), :] for at in range(8)], axis=0
    )
    diagonal = jnp.exp(start + order_f * lat_ref[16:24])
    zero = jnp.zeros((8, total_lat), jnp.float32)

    def rung(degree_f, carry):
        previous, earlier, inverse = carry
        higher = degree_f > order_f
        numerator = jnp.maximum(4.0 * degree_f * degree_f - 1.0, 1.0)
        denominator = jnp.where(higher, degree_f * degree_f - order_f * order_f, 1.0)
        mixed = lax.rsqrt(numerator * denominator)
        factor = numerator * mixed
        back_factor = denominator * mixed
        raised = factor * (sin_lat * previous - inverse * earlier)
        current = jnp.where(degree_f == order_f, diagonal, jnp.where(higher, raised, 0.0))
        return current, previous, jnp.where(higher, back_factor, 0.0)

    def ladder(block, carry):
        for at in range(8):
            degree = block * 8 + at
            carry = rung(degree.astype(jnp.float32), carry)
            table[pl.ds(pl.multiple_of(degree * 8, 8), 8), :] = carry[0]
        return carry

    lax.fori_loop(0, NN // 8, ladder, (zero, zero, zero))

    ones = jnp.ones((8, 128), jnp.float32)
    for chunk in range(chunks):
        theta_copy(chunk).wait()
        totals = []
        for at in range(rows):
            row = chunk * rows + at
            total = theta[row, :, 0:128]
            for tile in range(1, cells // 128):
                total = total + theta[row, :, tile * 128:(tile + 1) * 128]
            totals.append(total)
        sums = lax.dot_general(
            ones, jnp.concatenate(totals, axis=0), (((1,), (1,)), ((), ())),
            precision=HIGHEST, preferred_element_type=jnp.float32,
        )
        for at in range(rows):
            row = chunk * rows + at
            heat[row:row + 1, :] = sums[0:1, at * lat_local:(at + 1) * lat_local]
    forward_copy.wait()
    back_copy.wait()
    heating = heat[...]
    coefs = jnp.dot(forward[...], heating, precision=HIGHEST, preferred_element_type=jnp.float32)
    send1[...] = coefs.reshape(peers, 16, lat_local)
    pl.semaphore_wait(barrier, peers - 1)

    def first(offset):
        peer, device = place(offset)
        return pltpu.make_async_remote_copy(
            src_ref=send1.at[peer], dst_ref=recv1.at[me],
            send_sem=s1_sem.at[peer], recv_sem=r1_sem.at[me],
            device_id=device, device_id_type=MESH,
        )

    def first_arrival(offset):
        peer, device = place(offset)
        return pltpu.make_async_remote_copy(
            src_ref=send1.at[peer], dst_ref=recv1.at[peer],
            send_sem=s1_sem.at[peer], recv_sem=r1_sem.at[peer],
            device_id=device, device_id_type=MESH,
        )

    def second(offset):
        peer, device = place(offset)
        return pltpu.make_async_remote_copy(
            src_ref=send2.at[lax.rem(peer, lat_devices)], dst_ref=recv2.at[me],
            send_sem=s2_sem.at[peer], recv_sem=r2_sem.at[me],
            device_id=device, device_id_type=MESH,
        )

    def second_arrival(offset):
        peer, device = place(offset)
        return pltpu.make_async_remote_copy(
            src_ref=send2.at[lax.rem(peer, lat_devices)], dst_ref=recv2.at[peer],
            send_sem=s2_sem.at[peer], recv_sem=r2_sem.at[peer],
            device_id=device, device_id_type=MESH,
        )

    def for_peers(act):
        def step(offset, carry):
            act(offset)
            return carry
        lax.fori_loop(1, peers, step, 0)

    for_peers(lambda offset: first(offset).start())
    recv1[me] = send1[me]
    count_bounds(counts_ref, least_ref, most_ref, 128 // levels)
    trips_ref[...] = spread_columns(counts_ref[...].astype(jnp.float32), levels, HIGHEST)
    for_peers(lambda offset: first_arrival(offset).wait_recv())
    halves = []
    for half in range(lat_devices):
        total = recv1[half]
        for at in range(1, lon_devices):
            total = total + recv1[at * lat_devices + half]
        halves.append(total)
    whole = jnp.concatenate(halves, axis=1)
    weighted = whole * jnp.concatenate([weight, weight], axis=0)

    width = table.shape[0]
    spectrum = lax.dot_general(
        weighted, table[...], (((1,), (1,)), ((), ())),
        precision=HIGHEST, preferred_element_type=jnp.float32,
    )
    lane = lax.broadcasted_iota(jnp.int32, (16, width), 1)
    own = lax.rem(lax.broadcasted_iota(jnp.int32, (16, width), 0), 8)
    kept = jnp.full((16, width), -1, jnp.int32)
    for at in range(per_peer):
        kept = jnp.where(own == at, trunc_ref[me * per_peer + at], kept)
    keep = (lane % 8 == own) & (lane // 8 <= kept)
    filtered = jnp.dot(
        jnp.where(keep, spectrum, 0.0), table[...],
        precision=HIGHEST, preferred_element_type=jnp.float32,
    )
    for half in range(lat_devices):
        send2[half] = filtered[:, half * lat_local:(half + 1) * lat_local]
    for_peers(lambda offset: second(offset).start())
    recv2[me] = send2[lat]
    for_peers(lambda offset: second_arrival(offset).wait_recv())
    gathered = recv2[...].reshape(peers * 16, lat_local)
    forcing = jnp.dot(
        back[...], gathered, precision=HIGHEST, preferred_element_type=jnp.float32
    )
    heat_ref[...] = spread_columns(forcing, levels, HIGHEST)
    for_peers(lambda offset: first(offset).wait_send())
    for_peers(lambda offset: second(offset).wait_send())


def spectral_forcing(cloud_state, counts, truncation, levels):
    lon_devices = lax.axis_size("lon")
    lat_devices = lax.axis_size("lat")
    peers = lon_devices * lat_devices
    _, lon_local, lat_local, cells = cloud_state.shape
    total_lon, total_lat = lon_local * lon_devices, lat_local * lat_devices
    modes = truncation.shape[0]
    chunks = 8 if lon_local % 8 == 0 else 1
    forward, back = wave_tables(total_lon, lon_devices, modes, peers, 1.0 / (total_lon * cells))
    lat_consts = np.concatenate(
        [latitude_rows(total_lat).reshape(24, total_lat), order_starts(modes, total_lat)]
    )
    vmem = pl.BlockSpec(memory_space=pltpu.VMEM)
    hbm = pl.BlockSpec(memory_space=pl.ANY)
    return pl.pallas_call(
        functools.partial(spectral_kernel, lon_devices, lat_devices, modes, chunks, levels),
        out_shape=(
            jax.ShapeDtypeStruct((lat_local, lon_local * levels), jnp.float32),
            jax.ShapeDtypeStruct((lat_local, lon_local * levels), jnp.float32),
            jax.ShapeDtypeStruct((lon_local, lat_local), jnp.int32),
            jax.ShapeDtypeStruct((lon_local, lat_local), jnp.int32),
        ),
        in_specs=[pl.BlockSpec(memory_space=pltpu.SMEM), hbm, hbm, hbm, vmem, vmem],
        out_specs=(vmem,) * 4,
        scratch_shapes=[
            pltpu.VMEM((lon_local, lat_local, cells), jnp.float32),
            pltpu.VMEM((NN * 8, total_lat), jnp.float32),
            pltpu.VMEM((lon_local, lat_local), jnp.float32),
            pltpu.VMEM(forward.shape[1:], jnp.float32),
            pltpu.VMEM(back.shape[1:], jnp.float32),
            pltpu.VMEM((peers, 16, lat_local), jnp.float32),
            pltpu.VMEM((peers, 16, lat_local), jnp.float32),
            pltpu.VMEM((lat_devices, 16, lat_local), jnp.float32),
            pltpu.VMEM((peers, 16, lat_local), jnp.float32),
            pltpu.SemaphoreType.DMA((chunks,)),
            pltpu.SemaphoreType.DMA((2,)),
            pltpu.SemaphoreType.DMA((peers,)),
            pltpu.SemaphoreType.DMA((peers,)),
            pltpu.SemaphoreType.DMA((peers,)),
            pltpu.SemaphoreType.DMA((peers,)),
        ],
        compiler_params=pltpu.CompilerParams(
            collective_id=0, has_side_effects=True, vmem_limit_bytes=60 << 20
        ),
        name="spectral",
    )(truncation, cloud_state, jnp.asarray(forward), jnp.asarray(back), jnp.asarray(lat_consts), counts)


def swap_blocks(cols, low_half, even):
    mixed = jnp.where(even, cols[0], cols[2])
    other = jnp.where(even, cols[2], cols[0])
    moved = pltpu.roll(jnp.where(low_half, other, mixed), 64, 1)
    a0 = jnp.where(low_half, mixed, moved)
    b0 = jnp.where(low_half, moved, other)
    moved = pltpu.roll(jnp.where(low_half, cols[3], cols[1]), 64, 1)
    a1 = jnp.where(low_half, cols[1], moved)
    b1 = jnp.where(low_half, moved, cols[3])
    out = []
    for a, b in ((a0, a1), (b0, b1)):
        moved = pltpu.roll(jnp.where(even, b, a), 32, 1)
        out += [jnp.where(even, a, moved), jnp.where(even, moved, b)]
    return out


def cloud_kernel(
    lat_blocks, least_ref, most_ref, courant_ref, profile_ref, heat_ref, trips_ref, x_ref,
    o_ref, u_ref, w_ref, const_ref,
):
    chunk = pl.program_id(0)

    @pl.when(chunk == 0)
    def _():
        fill_constants(const_ref, courant_ref, profile_ref)

    group = x_ref.shape[1] // lat_blocks
    tiles = x_ref.shape[2] // 8
    cells = tiles * group
    lane = lax.broadcasted_iota(jnp.int32, (8, 128), 1)
    low_half = lane < 64
    even = (lane // 32) % 2 == 0
    kappa = 0.275 / 0.725

    def batch(jb, carry):
        least = least_ref[chunk * group, jb * 8]
        most = most_ref[chunk * group, jb * 8]
        lats = pl.ds(pl.multiple_of(jb * 8, 8), 8)
        heat = heat_ref[lats, :] * const_ref[1]
        trips = trips_ref[lats, :].astype(jnp.int32)
        rho = const_ref[0]
        us = []
        for tile in range(tiles):
            u4, w4 = [], []
            for at in range(group):
                theta = x_ref[0, at * lat_blocks + jb, tile * 8:tile * 8 + 8, :]
                moist = x_ref[1, at * lat_blocks + jb, tile * 8:tile * 8 + 8, :]
                u4.append((10.0 / 0.725) * moist - (2.0 / 0.725) * theta - (10.0 / 0.725))
                w4.append(theta + 0.5 * moist)
            us += swap_blocks(u4, low_half, even)
            for at, value in enumerate(swap_blocks(w4, low_half, even)):
                w_ref[tile * group + at] = value

        def advance_u(masked, step, us):
            scale = const_ref[2 + 9 + step + 1]
            floor = scale * scale
            push = 2.0 * heat * scale
            active = step < trips
            out = []
            for at in range(cells):
                y = us[at] + rho * us[at - 1] - push
                z = y * y + floor
                value = y - kappa * (z * lax.rsqrt(z))
                out.append(jnp.where(active, value, us[at]) if masked else value)
            return tuple(out)

        def advance_w(masked, step, ws):
            active = step < trips
            out = []
            for at in range(cells):
                value = ws[at] + rho * ws[at - 1]
                out.append(jnp.where(active, value, ws[at]) if masked else value)
            return tuple(out)

        us = lax.fori_loop(0, least, functools.partial(advance_u, False), tuple(us))
        us = lax.fori_loop(least, most, functools.partial(advance_u, True), us)
        for at in range(cells):
            u_ref[at] = us[at]
        ws = tuple(w_ref[at] for at in range(cells))
        ws = lax.fori_loop(0, least, functools.partial(advance_w, False), ws)
        ws = lax.fori_loop(least, most, functools.partial(advance_w, True), ws)

        u_scale = const_ref[2 + 18 + 1]
        w_scale = const_ref[2 + 1]
        for count in range(2, 9):
            u_scale = jnp.where(trips == count, const_ref[2 + 18 + count], u_scale)
            w_scale = jnp.where(trips == count, const_ref[2 + count], w_scale)
        shift = trips.astype(jnp.float32) * heat * (1.0 / 1.1) - 0.5 / 1.1
        u_theta = u_scale * (0.5 / 1.1)
        for tile in range(tiles):
            thetas, moists = [], []
            for at in range(group):
                u, w = u_ref[tile * group + at], ws[tile * group + at]
                theta = w_scale * w - u_theta * u + shift
                thetas.append(theta)
                moists.append(u_scale * u + (1.0 + 0.2 * theta))
            thetas = swap_blocks(thetas, low_half, even)
            moists = swap_blocks(moists, low_half, even)
            for at in range(group):
                o_ref[0, at * lat_blocks + jb, tile * 8:tile * 8 + 8, :] = thetas[at]
                o_ref[1, at * lat_blocks + jb, tile * 8:tile * 8 + 8, :] = moists[at]
        return carry

    lax.fori_loop(0, lat_blocks, batch, 0)


def fill_constants(const_ref, courant_ref, profile_ref):
    levels = courant_ref.shape[1]
    rate = jnp.concatenate([courant_ref[...]] * (128 // levels), axis=1)
    keep = jnp.broadcast_to(1.0 - rate, (8, 128))
    lower = 0.725 * keep
    const_ref[0] = (1.0 - keep) / keep
    const_ref[1] = profile_ref[...]
    first = 2
    for base, value in ((keep, 1.0 / 1.1), (1.0 / lower, 1.0), (lower, 0.0725)):
        power = jnp.full((8, 128), value, jnp.float32)
        for at in range(9):
            const_ref[first + at] = power
            power = power * base
        first += 9


def shards(cloud_state, counts, courant, truncation):
    fields, lon_local, lat_local, cells = cloud_state.shape
    levels = courant.shape[0]
    rows = 128 // levels
    heat, trips, least, most = spectral_forcing(cloud_state, counts, truncation, levels)
    heights = COUPLE * np.sin(np.pi * (np.arange(levels) + 0.5) / levels)
    profile = np.tile(heights, (8, 128 // levels)).astype(np.float32)
    lat_blocks, tiles = lat_local // 8, cells // 128
    view = cloud_state.reshape(fields, lon_local, lat_blocks, 8, tiles, 128)
    view = view.transpose(0, 1, 2, 4, 3, 5).reshape(fields, lon_local * lat_blocks, tiles * 8, 128)
    block = pl.BlockSpec((fields, rows * lat_blocks, tiles * 8, 128), lambda i: (0, i, 0, 0))
    smem = pl.BlockSpec(memory_space=pltpu.SMEM)
    updated = pl.pallas_call(
        functools.partial(cloud_kernel, lat_blocks),
        out_shape=jax.ShapeDtypeStruct(view.shape, jnp.float32),
        grid=(lon_local // rows,),
        in_specs=[
            smem, smem, pl.BlockSpec(memory_space=pltpu.VMEM), pl.BlockSpec(memory_space=pltpu.VMEM),
            pl.BlockSpec((lat_local, 128), lambda i: (0, i)),
            pl.BlockSpec((lat_local, 128), lambda i: (0, i)),
            block,
        ],
        out_specs=block,
        scratch_shapes=[pltpu.VMEM((cells // levels, 8, 128), jnp.float32)] * 2 + [
            pltpu.VMEM((29, 8, 128), jnp.float32)
        ],
        compiler_params=pltpu.CompilerParams(vmem_limit_bytes=60 << 20),
        name="cloud",
    )(
        least, most, courant.reshape(1, levels), jnp.asarray(profile), heat, trips, view
    )
    updated = updated.reshape(fields, lon_local, lat_blocks, tiles, 8, 128).transpose(0, 1, 2, 4, 3, 5)
    return updated.reshape(cloud_state.shape)


def solution(mesh):
    return jax.shard_map(
        shards,
        mesh=mesh,
        in_specs=(P("grp", "lon", "lat", None), P(("grp", "lon"), "lat"), P(), P()),
        out_specs=P("grp", "lon", "lat", None),
        check_vma=False,
    )
```
